32 devices in a mesh: row: 8 (over y, x, core), col: 4 (over z).
Axes of the slice: x: 2, y: 2, z: 4, core: 2. Of those that a mesh axis runs over, the one named last changes fastest.
Arguments:
- front_first: float32 [8, 8, 128, 4, 16, 128], P('row', None, None, 'col'), as said below
- front_second: float32 [8, 8, 128, 4, 16, 128], P('row', None, None, 'col'), as said below
- front_third: float32 [8, 8, 128, 4, 16, 128], P('row', None, None, 'col'), as said below
- map_second: int32 [60], replicated, may hold values from 0 to 63, as said below
- map_third: int32 [60], replicated, may hold values from 0 to 63, as said below
Outputs:
- lower_first: float32 [8, 8, 128, 512], P('row')
- lower_second: float32 [8, 8, 128, 512], P('row')
- lower_third: float32 [8, 8, 128, 512], P('row')
- schur_third: float32 [8, 8, 128, 4, 16, 128], P('row', None, None, 'col')
The draws below stay inside these ranges and needn't reach their ends.
Inputs may be any that keep to these rules, and one draw needn't show every extreme that they name: `map_second`: strictly increasing; the first entry is 0 and the last is 63. `map_third`: strictly increasing; the first entry is 0 and the last is 63. `front_first`: symmetric positive definite. `front_second`: symmetric positive definite. `front_third`: symmetric positive definite.
All inputs are finite; a program needn't handle non-finite values.
Results may differ from the reference program's by a relative error of at most 0.00012.
Values sent between devices are 32-bit elements; how exact they have to be, the bound alone decides.
A program may use at most 128 MiB of HBM per device.

```python
import math
import jax
import jax.numpy as jnp
from jax import lax

TILE = 128
PANEL = 512
PANELS = 1
FRONT = 8192
GRID_ROWS = 8
GRID_COLS = 4
TILES_ROW = 8
TILES_COL = 16
PIVOTS = 512
BLOCKS = 64
CHILD_BLOCKS = 60


def make_front(key):
    entries = jax.random.normal(key, (FRONT, PIVOTS), jnp.float32)
    factors = entries * (2.0 / math.sqrt(PIVOTS))
    product = jnp.dot(factors, factors.T, precision=lax.Precision.HIGHEST, preferred_element_type=jnp.float32)
    product = 0.5 * (product + product.T)
    diagonal_values = jax.random.uniform(jax.random.fold_in(key, 7), (FRONT,), jnp.float32, 1.0, 2.0)
    matrix = product + jnp.diag(diagonal_values)
    return matrix.reshape(TILES_ROW, GRID_ROWS, TILE, TILES_COL, GRID_COLS, TILE).transpose(1, 0, 2, 4, 3, 5)


def make_map(key):
    pivot_blocks = PIVOTS // TILE
    shuffled = jax.random.permutation(key, BLOCKS - 2) + 1
    skipped = shuffled[:pivot_blocks]
    block_ids = jnp.arange(BLOCKS, dtype=jnp.int32)
    skipped_mask = jnp.any(block_ids[:, None] == skipped[None, :], axis=1)
    ranking = block_ids + BLOCKS * skipped_mask.astype(jnp.int32)
    return jnp.argsort(ranking)[:BLOCKS - pivot_blocks].astype(jnp.int32)


def draw_front_first(key, part):
    return make_front(jax.random.fold_in(key, 1))


def draw_front_second(key, part):
    return make_front(jax.random.fold_in(key, 2))


def draw_front_third(key, part):
    return make_front(jax.random.fold_in(key, 3))


def draw_map_second(key, part):
    return make_map(jax.random.fold_in(key, 11))


def draw_map_third(key, part):
    return make_map(jax.random.fold_in(key, 12))


def setup_inputs(seed: int = 0) -> dict:
    key_of = jax.random.split(jax.random.key(seed), 6)
    front_first = draw_front_first(jax.random.fold_in(key_of[5], 71), 0)
    front_second = draw_front_second(jax.random.fold_in(key_of[5], 71), 0)
    front_third = draw_front_third(jax.random.fold_in(key_of[5], 71), 0)
    map_second = draw_map_second(jax.random.fold_in(key_of[5], 71), 0)
    map_third = draw_map_third(jax.random.fold_in(key_of[5], 71), 0)
    return dict(front_first=front_first, front_second=front_second, front_third=front_third, map_second=map_second, map_third=map_third)


def unpack(front):
    return front.transpose(1, 0, 2, 4, 3, 5).reshape(FRONT, FRONT)

def to_layout(matrix):
    return matrix.reshape(TILES_ROW, GRID_ROWS, TILE, TILES_COL, GRID_COLS, TILE).transpose(1, 0, 2, 4, 3, 5)

def rows_layout(lower_all):
    return lower_all.reshape(TILES_ROW, GRID_ROWS, TILE, PIVOTS).transpose(1, 0, 2, 3)

def factor(matrix):
    row_ids = jnp.arange(FRONT)
    panels = []
    for panel_step in range(PANELS):
        start = panel_step * PANEL
        diagonal = matrix[start:start + PANEL, start:start + PANEL]
        factor_block = jnp.linalg.cholesky(diagonal)
        inverse = lax.linalg.triangular_solve(factor_block, jnp.eye(PANEL, dtype=jnp.float32), left_side=True, lower=True)
        panel_now = jnp.dot(matrix[:, start:start + PANEL].astype(jnp.float32), inverse.T.astype(jnp.float32), precision=lax.Precision.HIGHEST, preferred_element_type=jnp.float32)
        panel_now = jnp.where((row_ids >= start)[:, None], panel_now, 0.0)
        matrix = matrix - jnp.dot(panel_now.astype(jnp.float32), panel_now.T.astype(jnp.float32), precision=lax.Precision.HIGHEST, preferred_element_type=jnp.float32)
        panels.append(panel_now)
    row_keep = row_ids >= PIVOTS
    schur = jnp.where(row_keep[:, None] & row_keep[None, :], matrix, 0.0)
    return (jnp.concatenate(panels, axis=1), schur)

def extend(parent, schur, block_map):
    pivot_blocks = PIVOTS // TILE
    child_tiles = schur.reshape(BLOCKS, TILE, BLOCKS, TILE)[pivot_blocks:, :, pivot_blocks:, :]
    placed_rows = jnp.zeros((BLOCKS, TILE, CHILD_BLOCKS, TILE), schur.dtype).at[block_map].set(child_tiles)
    placed = jnp.zeros((BLOCKS, TILE, BLOCKS, TILE), schur.dtype).at[:, :, block_map, :].set(placed_rows)
    return parent + placed.reshape(FRONT, FRONT)

def reference(front_first, front_second, front_third, map_second, map_third):
    lower_first, schur_first = factor(unpack(front_first))
    lower_second, schur_second = factor(extend(unpack(front_second), schur_first, map_second))
    lower_third, schur_third = factor(extend(unpack(front_third), schur_second, map_third))
    return (rows_layout(lower_first), rows_layout(lower_second), rows_layout(lower_third), to_layout(schur_third))
```

```python
import jax
import jax.numpy as jnp
from jax import lax
from jax.sharding import PartitionSpec as P

TILE = 128
PANEL = 512
PIVOTS = 512


def shifted(value, axis, steps):
    count = lax.axis_size(axis)
    pairs = [(source, (source + steps) % count) for source in range(count)]
    return lax.ppermute(value, axis, pairs)


def spread(block, axis, source):
    block = jnp.where(lax.axis_index(axis) == source, block, jnp.zeros_like(block))
    return lax.psum(block, axis)


def shift_rows(block_data, amount):
    return shifted(block_data, "row", amount)


def shift_cols(block_data, amount):
    return shifted(block_data, "col", amount)


def relocate(block_data, block_map, axis_dim, count, index, shifter):
    pivot_blocks = PIVOTS // TILE
    local_tiles = block_data.shape[axis_dim]
    child_start = jnp.arange(block_map.shape[0], dtype=jnp.int32) + pivot_blocks
    displacement = child_start - block_map
    local_pos = jnp.arange(local_tiles, dtype=jnp.int32) * count + index
    for bit_index in reversed(range(pivot_blocks.bit_length())):
        stride = 1 << bit_index
        high_part = displacement >> bit_index + 1 << bit_index + 1
        where_now = child_start - high_part
        moving_now = displacement >> bit_index & 1 == 1
        moving = jnp.any((where_now[None, :] == local_pos[:, None]) & moving_now[None, :], axis=1)
        if axis_dim == 0:
            tile_mask = moving[:, None, None, None]
        else:
            tile_mask = moving[None, None, :, None]
        sending = jnp.where(tile_mask, block_data, 0.0)
        staying = jnp.where(tile_mask, 0.0, block_data)
        full_turns = stride // count
        remainder = stride % count
        if remainder:
            arrived = shifter(sending, count - remainder)
        else:
            arrived = sending
        roll_amount = full_turns + (index + remainder >= count).astype(jnp.int32)
        arrived = jnp.roll(arrived, -roll_amount, axis=axis_dim)
        block_data = staying + arrived
    return block_data


def per_device(front_first, front_second, front_third, map_second, map_third):
    row_count = lax.axis_size("row")
    col_count = lax.axis_size("col")
    row_index = lax.axis_index("row")
    col_index = lax.axis_index("col")
    tiles_row = front_first.shape[1]
    tile_size = front_first.shape[2]
    tiles_col = front_first.shape[4]
    panel_tiles = PANEL // tile_size
    row_logical = (
        (jnp.arange(tiles_row, dtype=jnp.int32) * row_count + row_index)[:, None] * tile_size
        + jnp.arange(tile_size, dtype=jnp.int32)[None, :]
    ).reshape(-1)
    col_logical = (
        (jnp.arange(tiles_col, dtype=jnp.int32) * col_count + col_index)[:, None] * tile_size
        + jnp.arange(tile_size, dtype=jnp.int32)[None, :]
    ).reshape(-1)

    def local_form(front):
        return front.reshape(tiles_row, tile_size, tiles_col, tile_size)

    def factor_local(matrix):
        depth = -(-panel_tiles // col_count)
        gathered = lax.all_gather(matrix[:, :, :depth, :], "col")
        panel_cols = gathered.transpose(1, 2, 3, 0, 4).reshape(
            tiles_row * tile_size, depth * col_count * tile_size
        )[:, :PANEL]
        panel_tiled = panel_cols.reshape(tiles_row, tile_size, PANEL)
        depth = -(-panel_tiles // row_count)
        gathered = lax.all_gather(panel_tiled[:depth], "row")
        diagonal = gathered.transpose(1, 0, 2, 3).reshape(
            depth * row_count * tile_size, PANEL
        )[:PANEL]
        factor_block = jnp.linalg.cholesky(diagonal)
        inverse = lax.linalg.triangular_solve(
            factor_block, jnp.eye(PANEL, dtype=jnp.float32), left_side=True, lower=True
        )
        lower_panel = jnp.dot(
            panel_cols,
            inverse.T,
            precision=lax.Precision.HIGHEST,
            preferred_element_type=jnp.float32,
        )
        lower_panel = jnp.where((row_logical >= 0)[:, None], lower_panel, 0.0)
        received = []
        for member in range(row_count // col_count):
            got = spread(lower_panel, "row", member * col_count + col_index)
            received.append(got.reshape(tiles_row, tile_size, PANEL))
        column_side = jnp.stack(received, axis=1).reshape(tiles_col * tile_size, PANEL)
        update = jnp.dot(
            lower_panel,
            column_side.T,
            precision=lax.Precision.HIGHEST,
            preferred_element_type=jnp.float32,
        )
        matrix = matrix - update.reshape(tiles_row, tile_size, tiles_col, tile_size)
        row_keep = (row_logical >= PIVOTS).reshape(tiles_row, tile_size)
        col_keep = (col_logical >= PIVOTS).reshape(tiles_col, tile_size)
        schur = jnp.where(row_keep[:, :, None, None] & col_keep[None, None, :, :], matrix, 0.0)
        return (lower_panel, schur)

    def extend_local(parent, schur, block_map):
        half = tile_size // 2
        upper, under = schur[:, :half], schur[:, half:]
        upper = relocate(upper, block_map, 0, row_count, row_index, shift_rows)
        under = relocate(under, block_map, 2, col_count, col_index, shift_cols)
        upper = relocate(upper, block_map, 2, col_count, col_index, shift_cols)
        under = relocate(under, block_map, 0, row_count, row_index, shift_rows)
        return parent + jnp.concatenate([upper, under], axis=1)

    lower_first, schur_first = factor_local(local_form(front_first))
    lower_second, schur_second = factor_local(
        extend_local(local_form(front_second), schur_first, map_second)
    )
    lower_third, schur_third = factor_local(
        extend_local(local_form(front_third), schur_second, map_third)
    )
    out_shape = (1, tiles_row, tile_size, PIVOTS)
    return (
        lower_first.reshape(out_shape),
        lower_second.reshape(out_shape),
        lower_third.reshape(out_shape),
        schur_third.reshape(1, tiles_row, tile_size, 1, tiles_col, tile_size),
    )


def solution(mesh):
    return jax.shard_map(
        per_device,
        mesh=mesh,
        in_specs=(
            P("row", None, None, "col", None, None),
            P("row", None, None, "col", None, None),
            P("row", None, None, "col", None, None),
            P(),
            P(),
        ),
        out_specs=(
            P("row", None, None, None),
            P("row", None, None, None),
            P("row", None, None, None),
            P("row", None, None, "col", None, None),
        ),
        check_vma=False,
    )
```
